32 devices in a mesh: table: 4 (over y, x), fsdp: 8 (over z, core).
Axes of the slice: x: 2, y: 2, z: 4, core: 2. Of those that a mesh axis runs over, the one named last changes fastest.
Arguments:
- table_rows: bfloat16 [8, 2048, 128], P('fsdp', 'table'), may hold values from -6 to 6
- requests: int32 [8, 4, 4, 32], P('fsdp', 'table'), may hold values from -1 to 511, as said below
- bag_slots: int32 [8, 64, 26, 4], P('fsdp', 'table'), may hold values from -1 to 127, as said below
- pattern: int32 [64, 7], replicated, may hold values from 0 to 25, as said below
- tiles: bfloat16 [64, 7, 128, 128], P('table', None, 'fsdp'), may hold values from -0.1875 to 0.1875
- cotangent: bfloat16 [8, 64, 8192], P('fsdp', None, 'table'), may hold values from -6 to 6
Outputs:
- activation: bfloat16 [8, 64, 8192], P('fsdp', None, 'table')
- row_grads: float32 [8, 2048, 128], P('fsdp', 'table')
The draws below stay inside these ranges and needn't reach their ends.
Inputs may be any that keep to these rules, and one draw needn't show every extreme that they name: Each list requests[f, o, d] holds between 8 and 32 distinct row indices followed by -1 in its remaining slots; in each group one owner's lists are all full. `bag_slots`: every entry that is not -1 names a slot that holds a row (not -1 in requests); the first entry of each bag is never -1 and -1 entries come only after all others. `pattern`: the 7 numbers of a column block are distinct.
All inputs are finite; a program needn't handle non-finite values.
Results may differ from the reference program's by a relative error of at most 0.012.
Values may be sent and summed in bfloat16 or wider, within the bound.
A program may use at most 64 MiB of HBM per device.

```python
import jax
import jax.numpy as jnp
from jax import lax

EMB = 128
FEAT = 26
COLS = 8192
NZ = 7
BAG = 4
B_DEV = 16
ROWS_DEV = 512
CAP = 32
COLBLK = 64
GROUP = 64
N_TABLE = 4
N_FSDP = 8


def counts_table(key):
    base = jax.random.randint(jax.random.fold_in(key, 11), (N_FSDP, N_TABLE, N_TABLE), CAP // 4, CAP + 1)
    busiest = jax.random.randint(jax.random.fold_in(key, 12), (N_FSDP, 1, 1), 0, N_TABLE)
    owner_ids = jnp.arange(N_TABLE, dtype=jnp.int32)[None, :, None]
    return jnp.where(owner_ids == busiest, CAP, base).astype(jnp.int32)


def draw_requests(key, part):
    counts = counts_table(key)
    key = jax.random.fold_in(key, 1)
    subkeys = jax.random.split(key, N_FSDP * N_TABLE * N_TABLE)
    picks = jax.vmap(lambda subkey: jax.random.permutation(subkey, ROWS_DEV)[:CAP])(subkeys)
    picks = picks.reshape(N_FSDP, N_TABLE, N_TABLE, CAP).astype(jnp.int32)
    slot_ids = jnp.arange(CAP, dtype=jnp.int32)[None, None, None, :]
    return jnp.where(slot_ids < counts[..., None], picks, -1).astype(jnp.int32)


def draw_bag_slots(key, part):
    counts = counts_table(key)
    key = jax.random.fold_in(key, 2)
    first_key, second_key, third_key = jax.random.split(key, 3)
    shape = (N_FSDP, N_TABLE * B_DEV, FEAT, BAG)
    owner = jax.random.randint(first_key, shape, 0, N_TABLE)
    dest = (jnp.arange(N_TABLE * B_DEV, dtype=jnp.int32) // B_DEV)[None, :, None, None]
    group_ids = jnp.arange(N_FSDP, dtype=jnp.int32)[:, None, None, None]
    live_count = counts[group_ids, owner, dest]
    slot = jax.random.randint(second_key, shape, 0, 1 << 20) % live_count
    length = jax.random.randint(third_key, (N_FSDP, N_TABLE * B_DEV, FEAT, 1), 1, BAG + 1)
    entry = jnp.arange(BAG, dtype=jnp.int32)[None, None, None, :]
    return jnp.where(entry < length, owner * CAP + slot, -1).astype(jnp.int32)


def draw_pattern(key, part):
    key = jax.random.fold_in(key, 3)
    subkeys = jax.random.split(key, COLBLK)
    picks = jax.vmap(lambda subkey: jax.random.permutation(subkey, FEAT)[:NZ])(subkeys)
    return picks.astype(jnp.int32)


def levels(rng, shape, cuts, low, high):
    loudness, own = 1.0, jax.random.fold_in(rng, 6)
    for axis_at, shards_of in cuts:
        steps = jnp.exp(jax.random.uniform(jax.random.fold_in(own, axis_at), (shards_of,), jnp.float32, low / len(cuts), high / len(cuts)))
        loudness = loudness * jnp.repeat(steps, shape[axis_at] // shards_of).reshape([-1 if axis == axis_at else 1 for axis in range(len(shape))])
    return loudness


def noise(key, extent, scale, reach, pieces=(), kind=jnp.bfloat16):
    values = scale * jax.random.normal(key, extent, jnp.float32)
    if pieces:
        values = values * levels(key, extent, pieces, -0.22, 0.18)
    return jnp.clip(values, -reach, reach).astype(kind)


def setup_inputs(seed: int = 0) -> dict:
    splits = jax.random.split(jax.random.key(seed), 7)
    table_rows = noise(splits[0], (N_FSDP, N_TABLE * ROWS_DEV, EMB), 1.0, 6.0, ((0, 8), (1, 4)))
    requests = draw_requests(jax.random.fold_in(splits[6], 71), 0)
    bag_slots = draw_bag_slots(jax.random.fold_in(splits[6], 71), 0)
    pattern = draw_pattern(jax.random.fold_in(splits[6], 71), 0)
    tiles = noise(splits[4], (COLBLK, NZ, EMB, EMB), (NZ * EMB) ** -0.5, 0.1875, ((0, 4), (2, 8)))
    cotangent = noise(splits[5], (N_FSDP, GROUP, COLS), 1.0, 6.0, ((0, 8), (2, 4)))
    return {"table_rows": table_rows, "requests": requests, "bag_slots": bag_slots, "pattern": pattern, "tiles": tiles, "cotangent": cotangent}


def one_group(table_group, request_group, bag_group, cotangent_group, pattern, tiles):
    owners = request_group.shape[0]
    is_live = request_group >= 0
    safe_req = jnp.where(is_live, request_group, 0).astype(jnp.int32)
    sent = jax.vmap(lambda table_one, index_one: jnp.take(table_one, index_one, axis=0))(table_group, safe_req)
    sent = jnp.where(is_live[..., None], sent, jnp.zeros_like(sent))
    received = jnp.transpose(sent, (1, 0, 2, 3)).reshape(owners, owners * CAP, EMB)
    bag_live = bag_group >= 0
    safe_bag = jnp.where(bag_live, bag_group, 0).astype(jnp.int32).reshape(owners, B_DEV * FEAT * BAG)
    values = jax.vmap(lambda slot_rows, index_one: jnp.take(slot_rows, index_one, axis=0))(received, safe_bag)
    values = values.reshape(GROUP, FEAT, BAG, EMB).astype(jnp.float32)
    values = jnp.where(bag_live[..., None], values, jnp.float32(0.0))
    pooled = jnp.sum(values, axis=2).astype(jnp.bfloat16)
    picked = jnp.take(pooled, pattern, axis=1)
    pre_act = jnp.einsum('gnie,niej->gnj', picked.astype(jnp.float32), tiles.astype(jnp.float32))
    activation = jax.nn.silu(pre_act).astype(jnp.bfloat16).reshape(GROUP, COLS)
    sigmoid_v = jax.nn.sigmoid(pre_act)
    upstream = cotangent_group.reshape(GROUP, COLBLK, EMB).astype(jnp.float32)
    grad_pre = (upstream * sigmoid_v * (1.0 + pre_act * (1.0 - sigmoid_v))).astype(jnp.bfloat16)
    grad_picked = jnp.einsum('gnj,niej->gnie', grad_pre.astype(jnp.float32), tiles.astype(jnp.float32))
    per_shard = (COLBLK // N_TABLE) * NZ
    grad_picked = grad_picked.reshape(GROUP, N_TABLE, per_shard, EMB)
    onehot = (pattern.reshape(N_TABLE, per_shard)[..., None] == jnp.arange(FEAT, dtype=jnp.int32)).astype(jnp.float32)
    partial_value = jnp.einsum('gtme,tmf->gtfe', grad_picked, onehot, precision=lax.Precision.HIGHEST)
    partial_value = partial_value.astype(jnp.bfloat16).astype(jnp.float32)
    grad_pooled = jnp.sum(partial_value, axis=1)
    spread = jnp.broadcast_to(grad_pooled[:, :, None, :], (GROUP, FEAT, BAG, EMB))
    spread = jnp.where(bag_live[..., None], spread, jnp.float32(0.0)).reshape(owners, B_DEV * FEAT * BAG, EMB)
    segment_ids = jnp.where(bag_live, bag_group, owners * CAP).astype(jnp.int32).reshape(owners, B_DEV * FEAT * BAG)
    slot_grads = jax.vmap(lambda data, ids: jax.ops.segment_sum(data, ids, num_segments=owners * CAP + 1))(spread, segment_ids)
    slot_grads = slot_grads[:, :owners * CAP].reshape(owners, owners, CAP, EMB)
    slot_grads = jnp.transpose(slot_grads, (1, 0, 2, 3)).reshape(owners, owners * CAP, EMB)
    row_ids = jnp.where(is_live, request_group, ROWS_DEV).astype(jnp.int32).reshape(owners, owners * CAP)
    row_grads = jax.vmap(lambda data, ids: jax.ops.segment_sum(data, ids, num_segments=ROWS_DEV + 1))(slot_grads, row_ids)
    row_grads = row_grads[:, :ROWS_DEV].reshape(owners * ROWS_DEV, EMB)
    return activation, row_grads


def reference(table_rows, requests, bag_slots, pattern, tiles, cotangent):
    table_split = table_rows.reshape(N_FSDP, N_TABLE, ROWS_DEV, EMB)

    def per_group(inputs):
        table_group, request_group, bag_group, cotangent_group = inputs
        return one_group(table_group, request_group, bag_group, cotangent_group, pattern, tiles)

    activation, row_grads = lax.map(per_group, (table_split, requests, bag_slots, cotangent))
    return (activation, row_grads)
```

```python
import functools

import jax
import jax.numpy as jnp
from jax import lax
from jax.experimental import pallas as pl
from jax.experimental.pallas import tpu as pltpu
from jax.sharding import PartitionSpec as P

MESH = pl.DeviceIdType.MESH
F32 = jnp.float32
BF16 = jnp.bfloat16
TILE_ROWS = 16
VMEM_LIMIT = 48 * 1024 * 1024
CHUNKS = 4


def local(table_rows, requests, bag_slots, pattern, tiles, cotangent):
    table_shard = table_rows[0]
    row_count = table_shard.shape[0]
    emb_width = table_shard.shape[1]
    request_list = requests[0, 0]
    peer_count = request_list.shape[0]
    slot_cap = request_list.shape[1]
    is_live = request_list >= 0
    sent_rows = jnp.take(table_shard, jnp.where(is_live, request_list, 0), axis=0)
    sent_rows = jnp.where(is_live[..., None], sent_rows, jnp.zeros_like(sent_rows))
    received = lax.all_to_all(sent_rows, "table", split_axis=0, concat_axis=0, tiled=True)
    slot_rows = received.reshape(peer_count * slot_cap, emb_width)
    bag_index = bag_slots[0]
    samples = bag_index.shape[0]
    feat_count = bag_index.shape[1]
    bag_depth = bag_index.shape[2]
    bag_live = bag_index >= 0
    values = jnp.take(slot_rows, jnp.where(bag_live, bag_index, 0).reshape(-1), axis=0)
    values = values.reshape(samples, feat_count, bag_depth, emb_width).astype(jnp.float32)
    values = jnp.where(bag_live[..., None], values, jnp.float32(0.0))
    pooled = jnp.sum(values, axis=2).astype(jnp.bfloat16)
    col_blocks = tiles.shape[0]
    per_block = tiles.shape[1]
    my_index = lax.axis_index("table")
    own_pattern = lax.dynamic_slice_in_dim(pattern, my_index * col_blocks, col_blocks, 0)
    group_rows = cotangent.shape[1]
    gathered = lax.all_gather(pooled, "table", axis=0, tiled=True)
    picked = jnp.take(gathered, own_pattern.reshape(-1), axis=1)
    picked = picked.reshape(group_rows, col_blocks, per_block * emb_width)
    full_tiles = lax.all_gather(tiles, "fsdp", axis=2, tiled=True)
    weights = full_tiles.reshape(col_blocks, per_block * emb_width, emb_width)
    pre_act = jnp.einsum("gck,ckj->gcj", picked, weights, preferred_element_type=jnp.float32)
    activation = (
        jax.nn.silu(pre_act).astype(jnp.bfloat16).reshape(1, group_rows, col_blocks * emb_width)
    )
    sigmoid_v = jax.nn.sigmoid(pre_act)
    upstream = cotangent[0].reshape(group_rows, col_blocks, emb_width).astype(jnp.float32)
    grad_pre = (upstream * sigmoid_v * (1.0 + pre_act * (1.0 - sigmoid_v))).astype(jnp.bfloat16)
    grad_picked = jnp.einsum("gcj,ckj->gck", grad_pre, weights, preferred_element_type=jnp.float32)
    grad_picked = grad_picked.reshape(group_rows, col_blocks * per_block, emb_width)
    own_flat = own_pattern.reshape(-1)
    onehot = (own_flat[:, None] == jnp.arange(feat_count, dtype=jnp.int32)[None, :]).astype(
        jnp.float32
    )
    partial_value = jnp.einsum("gme,mf->gfe", grad_picked, onehot, precision=lax.Precision.HIGHEST)
    grad_pooled = lax.psum_scatter(
        partial_value.astype(jnp.bfloat16), "table", scatter_dimension=0, tiled=True
    ).astype(jnp.float32)
    spread = jnp.broadcast_to(
        grad_pooled[:, :, None, :], (samples, feat_count, bag_depth, emb_width)
    )
    spread = jnp.where(bag_live[..., None], spread, jnp.float32(0.0)).reshape(-1, emb_width)
    segment_ids = jnp.where(bag_live, bag_index, peer_count * slot_cap).reshape(-1)
    slot_grads = jax.ops.segment_sum(spread, segment_ids, num_segments=peer_count * slot_cap + 1)
    slot_grads = slot_grads[: peer_count * slot_cap].reshape(peer_count, slot_cap, emb_width)
    returned = lax.all_to_all(
        slot_grads.astype(jnp.bfloat16), "table", split_axis=0, concat_axis=0, tiled=True
    ).astype(slot_grads.dtype)
    row_ids = jnp.where(is_live, request_list, row_count).reshape(-1)
    row_grads = jax.ops.segment_sum(
        returned.reshape(-1, emb_width), row_ids, num_segments=row_count + 1
    )
    row_grads = row_grads[:row_count].reshape(1, row_count, emb_width)
    return (activation, row_grads)


def contract(lhs, rhs, lhs_dim, rhs_dim):
    return lax.dot_general(
        lhs, rhs, (((lhs_dim,), (rhs_dim,)), ((), ())), preferred_element_type=F32
    )


def body(
    n_table,
    n_fsdp,
    chunks,
    table_ref,
    req_ref,
    bag_ref,
    pattern_ref,
    tiles_ref,
    cot_ref,
    act_ref,
    rows_ref,
    w,
    cot,
    act,
    req_row,
    bag_rows,
    pick,
    counts,
    sent,
    received,
    spread,
    pooled,
    products,
    total,
    part,
    parts_in,
    back,
    back_in,
    plan,
    plan_s,
    local_sem,
    w_send,
    w_recv,
    t_send,
    t_recv,
):
    col_blocks, per_block, tile_rows, emb = tiles_ref.shape
    step = col_blocks // chunks
    lines = n_fsdp // 2
    samples, depth, feats = bag_ref.shape[1:]
    slot_cap = req_ref.shape[3]
    slots = n_table * slot_cap
    group = cot_ref.shape[1]
    row_count = table_ref.shape[1]
    pad = bag_rows.shape[2] // (samples // bag_rows.shape[0])

    me = lax.axis_index("table")
    mine = lax.axis_index("fsdp")
    z = mine // 2
    core = mine % 2
    sibling = 2 * z + 1 - core

    barrier = pltpu.get_barrier_semaphore()
    for d in range(1, n_table):
        pl.semaphore_signal(
            barrier, inc=1, device_id={"table": lax.rem(me + d, n_table)}, device_id_type=MESH
        )
    pl.semaphore_signal(barrier, inc=1, device_id={"fsdp": sibling}, device_id_type=MESH)

    @pl.when(z > 0)
    def _():
        pl.semaphore_signal(barrier, inc=1, device_id={"fsdp": mine - 2}, device_id_type=MESH)

    @pl.when(z < lines - 1)
    def _():
        pl.semaphore_signal(barrier, inc=1, device_id={"fsdp": mine + 2}, device_id_type=MESH)

    own_tiles = pltpu.make_async_copy(
        tiles_ref,
        w.at[:, :, pl.ds(pl.multiple_of(mine * tile_rows, tile_rows), tile_rows), :],
        local_sem.at[0],
    )
    own_tiles.start()
    own_cot = pltpu.make_async_copy(cot_ref.at[0], cot, local_sem.at[1])
    own_cot.start()

    neighbours = jnp.where(z > 0, 1, 0) + jnp.where(z < lines - 1, 1, 0)
    pl.semaphore_wait(barrier, n_table + neighbours)

    def slot(chunk, source):
        at = pl.multiple_of(source * tile_rows, tile_rows)
        return w.at[pl.ds(chunk * step, step), :, pl.ds(at, tile_rows), :]

    def hop(way, chunk, line, target, own=False):
        source = 2 * line + core
        src = tiles_ref.at[pl.ds(chunk * step, step)] if own else slot(chunk, source)
        return pltpu.make_async_remote_copy(
            src_ref=src,
            dst_ref=slot(chunk, source),
            send_sem=w_send.at[way, chunk, line],
            recv_sem=w_recv.at[chunk, source],
            device_id={"fsdp": target},
            device_id_type=MESH,
        )

    def landed(chunk, source):
        pltpu.make_async_remote_copy(
            src_ref=slot(chunk, source),
            dst_ref=slot(chunk, source),
            send_sem=w_send.at[2, chunk, z],
            recv_sem=w_recv.at[chunk, source],
            device_id={"fsdp": sibling},
            device_id_type=MESH,
        ).wait_recv()

    def send_own(chunk, carry):
        @pl.when(z < lines - 1)
        def _():
            hop(0, chunk, z, mine + 2, True).start()

        @pl.when(z > 0)
        def _():
            hop(1, chunk, z, mine - 2, True).start()

        return carry

    lax.fori_loop(0, chunks, send_own, 0)

    def send_own_core(chunk, carry):
        hop(2, chunk, z, sibling, True).start()
        return carry

    lax.fori_loop(0, chunks, send_own_core, 0)

    def exchange(phase, source_of, target):
        copies = []
        for d in range(1, n_table):
            peer = lax.rem(me + d, n_table)
            copy = pltpu.make_async_remote_copy(
                src_ref=source_of(peer),
                dst_ref=target,
                send_sem=t_send.at[phase, d],
                recv_sem=t_recv.at[phase, d],
                device_id={"table": peer},
                device_id_type=MESH,
            )
            copy.start()
            copies.append(copy)
        return copies

    for d in range(n_table):
        req_row[:, d * slot_cap : (d + 1) * slot_cap] = req_ref[0, 0, d : d + 1, :]
    row_ids = lax.broadcasted_iota(jnp.int32, (row_count, slots), 0)
    pick[...] = jnp.where(row_ids == req_row[...], 1.0, 0.0).astype(BF16)
    sent[...] = (
        contract(pick[...], table_ref[0], 0, 0).astype(BF16).reshape(n_table, slot_cap, emb)
    )
    first = exchange(0, lambda peer: sent.at[peer], received.at[me])
    received[me] = sent[me]

    bag_rows[...] = jnp.full(bag_rows.shape, -1, jnp.int32)
    per_row = samples // bag_rows.shape[0]
    for s in range(samples):
        at = (s % per_row) * pad
        bag_rows[s // per_row, :, at : at + feats] = bag_ref[0, s]
    width = per_row * pad
    slot_ids = lax.broadcasted_iota(jnp.int32, (slots, width), 0)
    for g in range(bag_rows.shape[0]):
        rows = bag_rows[g]
        found = jnp.zeros((slots, width), F32)
        for k in range(depth):
            found = found + jnp.where(slot_ids == rows[k : k + 1, :], 1.0, 0.0)
        counts[:, g * width : (g + 1) * width] = found.astype(BF16)

    plan[...] = jnp.zeros(plan.shape, jnp.int32)
    feat_ids = lax.broadcasted_iota(jnp.int32, (plan.shape[0] - 8, pattern_ref.shape[1]), 0)
    inverse = jnp.full(feat_ids.shape, per_block, jnp.int32)
    for i in range(per_block):
        inverse = jnp.where(feat_ids == pattern_ref[i : i + 1, :], i, inverse)
    plan[0 : plan.shape[0] - 8, 0 : pattern_ref.shape[1]] = inverse
    plan[plan.shape[0] - 8 : plan.shape[0] - 8 + per_block, 0 : pattern_ref.shape[1]] = pattern_ref[
        ...
    ]
    to_scalar = pltpu.make_async_copy(plan, plan_s, local_sem.at[2])
    to_scalar.start()
    products[...] = jnp.zeros(products.shape, F32)

    for copy in first:
        copy.wait_recv()
    spread[...] = contract(counts[...], received[...].reshape(slots, emb), 0, 0)
    at_me = pl.ds(pl.multiple_of(me * samples, samples), samples)
    for j in range(feats):
        pooled[j, at_me, :] = spread[pl.ds(j, samples, stride=pad), :].astype(BF16)
    second = exchange(1, lambda peer: pooled.at[:, at_me, :], pooled.at[:, at_me, :])
    to_scalar.wait()
    own_cot.wait()
    own_tiles.wait()

    def arrive(chunk, distance):
        @pl.when(z >= distance)
        def _():
            landed(chunk, mine - 2 * distance)

            @pl.when(z < lines - 1)
            def _():
                hop(0, chunk, z - distance, mine + 2).start()

            hop(2, chunk, z - distance, sibling).start()

        @pl.when(z + distance < lines)
        def _():
            landed(chunk, mine + 2 * distance)

            @pl.when(z > 0)
            def _():
                hop(1, chunk, z + distance, mine - 2).start()

            hop(2, chunk, z + distance, sibling).start()

    for distance in range(1, lines - 1):
        lax.fori_loop(
            0, chunks, lambda chunk, carry, distance=distance: (arrive(chunk, distance), carry)[1], 0
        )
    for copy in second:
        copy.wait_recv()

    def work(chunk, carry):
        arrive(chunk, lines - 1)
        for line in range(lines):
            landed(chunk, 2 * line + 1 - core)
        for b in range(step):
            n = chunk * step + b
            picked = jnp.concatenate(
                [
                    pooled[plan_s[plan.shape[0] - 8 + i, me * col_blocks + n]]
                    for i in range(per_block)
                ],
                axis=1,
            )
            weights = w[n].reshape(per_block * emb, emb)
            pre = contract(picked, weights, 1, 0)
            sig = jax.nn.sigmoid(pre)
            columns = pl.ds(pl.multiple_of(n * emb, emb), emb)
            act[:, columns] = (pre * sig).astype(BF16)
            up = cot[:, columns].astype(F32)
            grad = (up * sig * (1.0 + pre * (1.0 - sig))).astype(BF16)
            back_rows = contract(grad, weights, 1, 1)
            for i in range(per_block):
                products[b, i] = back_rows[:, i * emb : (i + 1) * emb]

        def add(j, c):
            value = products[0, plan_s[j, me * col_blocks + chunk * step]]
            for b in range(1, step):
                value = value + products[b, plan_s[j, me * col_blocks + chunk * step + b]]
            total[j] = jnp.where(chunk == 0, value, total[j] + value)
            return c

        lax.fori_loop(0, feats, add, 0, unroll=2)
        return carry

    total[...] = jnp.zeros(total.shape, F32)
    lax.fori_loop(0, chunks, work, 0)
    act_out = pltpu.make_async_copy(act, act_ref.at[0], local_sem.at[3])
    act_out.start()

    part[...] = total[...].astype(BF16)
    third = exchange(
        2,
        lambda peer: part.at[:, pl.ds(pl.multiple_of(peer * samples, samples), samples), :],
        parts_in.at[me],
    )
    parts_in[me] = part[:, at_me, :]
    spread[...] = jnp.zeros(spread.shape, F32)
    for copy in third:
        copy.wait_recv()
    for j in range(feats):
        value = parts_in[0, j].astype(F32)
        for d in range(1, n_table):
            value = value + parts_in[d, j].astype(F32)
        spread[pl.ds(j, samples, stride=pad), :] = value
    grads = spread[...]
    high = grads.astype(BF16)
    low = (grads - high.astype(F32)).astype(BF16)
    slot_grads = contract(counts[...], high, 1, 0) + contract(counts[...], low, 1, 0)
    back[...] = slot_grads.astype(BF16).reshape(n_table, slot_cap, emb)
    fourth = exchange(3, lambda peer: back.at[peer], back_in.at[me])
    back_in[me] = back[me]
    for copy in fourth:
        copy.wait_recv()
    rows_ref[0] = contract(pick[...], back_in[...].reshape(slots, emb), 1, 0)

    for copies in (first, second, third, fourth):
        for copy in copies:
            copy.wait_send()

    def sent_all(chunk, carry):
        for line in range(lines):
            hop(2, chunk, line, sibling).wait_send()

            @pl.when((line <= z) & (z < lines - 1))
            def _():
                hop(0, chunk, line, mine + 2).wait_send()

            @pl.when((line >= z) & (z > 0))
            def _():
                hop(1, chunk, line, mine - 2).wait_send()

        return carry

    lax.fori_loop(0, chunks, sent_all, 0)
    act_out.wait()


def fused(n_table, n_fsdp, chunks, table_rows, requests, bag_slots, pattern, tiles, cotangent):
    col_blocks, per_block, tile_rows, emb = tiles.shape
    group = cotangent.shape[1]
    row_count = table_rows.shape[1]
    samples, feats, depth = bag_slots.shape[1:]
    slot_cap = requests.shape[3]
    slots = n_table * slot_cap
    lines = n_fsdp // 2
    pad = 32
    per_row = 128 // pad
    plan_rows = pad + 8
    vmem, anywhere = pl.BlockSpec(memory_space=pltpu.VMEM), pl.BlockSpec(memory_space=pl.ANY)
    return pl.pallas_call(
        functools.partial(body, n_table, n_fsdp, chunks),
        out_shape=(
            jax.ShapeDtypeStruct((1, group, col_blocks * emb), BF16),
            jax.ShapeDtypeStruct((1, row_count, emb), F32),
        ),
        in_specs=[vmem, vmem, vmem, vmem, anywhere, anywhere],
        out_specs=(anywhere, vmem),
        scratch_shapes=[
            pltpu.VMEM((col_blocks, per_block, tile_rows * n_fsdp, emb), BF16),
            pltpu.VMEM((group, col_blocks * emb), BF16),
            pltpu.VMEM((group, col_blocks * emb), BF16),
            pltpu.VMEM((1, slots), jnp.int32),
            pltpu.VMEM((samples // per_row, depth, per_row * pad), jnp.int32),
            pltpu.VMEM((row_count, slots), BF16),
            pltpu.VMEM((slots, samples * pad), BF16),
            pltpu.VMEM((n_table, slot_cap, emb), BF16),
            pltpu.VMEM((n_table, slot_cap, emb), BF16),
            pltpu.VMEM((samples * pad, emb), F32),
            pltpu.VMEM((feats, group, emb), BF16),
            pltpu.VMEM((col_blocks // chunks, per_block + 1, group, emb), F32),
            pltpu.VMEM((feats, group, emb), F32),
            pltpu.VMEM((feats, group, emb), BF16),
            pltpu.VMEM((n_table, feats, samples, emb), BF16),
            pltpu.VMEM((n_table, slot_cap, emb), BF16),
            pltpu.VMEM((n_table, slot_cap, emb), BF16),
            pltpu.VMEM((plan_rows, 128), jnp.int32),
            pltpu.SMEM((plan_rows, 128), jnp.int32),
            pltpu.SemaphoreType.DMA((4,)),
            pltpu.SemaphoreType.DMA((3, chunks, lines)),
            pltpu.SemaphoreType.DMA((chunks, n_fsdp)),
            pltpu.SemaphoreType.DMA((4, n_table)),
            pltpu.SemaphoreType.DMA((4, n_table)),
        ],
        compiler_params=pltpu.CompilerParams(
            collective_id=0, has_side_effects=True, vmem_limit_bytes=VMEM_LIMIT
        ),
    )(
        table_rows,
        requests,
        jnp.swapaxes(bag_slots, 2, 3),
        pattern.T,
        tiles,
        cotangent,
    )


def solution(mesh):
    n_table, n_fsdp = mesh.shape["table"], mesh.shape["fsdp"]
    in_specs = (
        P("fsdp", "table", None),
        P("fsdp", "table", None, None),
        P("fsdp", "table", None, None),
        P(),
        P("table", None, "fsdp", None),
        P("fsdp", None, "table"),
    )
    out_specs = (P("fsdp", None, "table"), P("fsdp", "table", None))

    def program(table_rows, requests, bag_slots, pattern, tiles, cotangent):
        col_blocks, _, tile_rows, emb = tiles.shape
        samples, feats = bag_slots.shape[1:3]
        whole = (
            tile_rows % TILE_ROWS == 0
            and samples % TILE_ROWS == 0
            and emb == 128
            and n_table * requests.shape[3] == 128
            and feats <= 32
            and n_fsdp % 2 == 0
            and col_blocks % CHUNKS == 0
        )
        if whole:
            run = functools.partial(fused, n_table, n_fsdp, CHUNKS)
        else:
            run = local
        return run(table_rows, requests, bag_slots, pattern, tiles, cotangent)

    return jax.shard_map(program, mesh=mesh, in_specs=in_specs, out_specs=out_specs, check_vma=False)
```

```python
import functools

import jax
import jax.numpy as jnp
from jax import lax
from jax.experimental import pallas as pl
from jax.experimental.pallas import tpu as pltpu
from jax.sharding import PartitionSpec as P

MESH = pl.DeviceIdType.MESH
F32 = jnp.float32
BF16 = jnp.bfloat16
TILE_ROWS = 16
VMEM_LIMIT = 64 * 1024 * 1024
CHUNKS = 4


def local(table_rows, requests, bag_slots, pattern, tiles, cotangent):
    table_shard = table_rows[0]
    row_count = table_shard.shape[0]
    emb_width = table_shard.shape[1]
    request_list = requests[0, 0]
    peer_count = request_list.shape[0]
    slot_cap = request_list.shape[1]
    is_live = request_list >= 0
    sent_rows = jnp.take(table_shard, jnp.where(is_live, request_list, 0), axis=0)
    sent_rows = jnp.where(is_live[..., None], sent_rows, jnp.zeros_like(sent_rows))
    received = lax.all_to_all(sent_rows, "table", split_axis=0, concat_axis=0, tiled=True)
    slot_rows = received.reshape(peer_count * slot_cap, emb_width)
    bag_index = bag_slots[0]
    samples = bag_index.shape[0]
    feat_count = bag_index.shape[1]
    bag_depth = bag_index.shape[2]
    bag_live = bag_index >= 0
    values = jnp.take(slot_rows, jnp.where(bag_live, bag_index, 0).reshape(-1), axis=0)
    values = values.reshape(samples, feat_count, bag_depth, emb_width).astype(jnp.float32)
    values = jnp.where(bag_live[..., None], values, jnp.float32(0.0))
    pooled = jnp.sum(values, axis=2).astype(jnp.bfloat16)
    col_blocks = tiles.shape[0]
    per_block = tiles.shape[1]
    my_index = lax.axis_index("table")
    own_pattern = lax.dynamic_slice_in_dim(pattern, my_index * col_blocks, col_blocks, 0)
    group_rows = cotangent.shape[1]
    gathered = lax.all_gather(pooled, "table", axis=0, tiled=True)
    picked = jnp.take(gathered, own_pattern.reshape(-1), axis=1)
    picked = picked.reshape(group_rows, col_blocks, per_block * emb_width)
    full_tiles = lax.all_gather(tiles, "fsdp", axis=2, tiled=True)
    weights = full_tiles.reshape(col_blocks, per_block * emb_width, emb_width)
    pre_act = jnp.einsum("gck,ckj->gcj", picked, weights, preferred_element_type=jnp.float32)
    activation = (
        jax.nn.silu(pre_act).astype(jnp.bfloat16).reshape(1, group_rows, col_blocks * emb_width)
    )
    sigmoid_v = jax.nn.sigmoid(pre_act)
    upstream = cotangent[0].reshape(group_rows, col_blocks, emb_width).astype(jnp.float32)
    grad_pre = (upstream * sigmoid_v * (1.0 + pre_act * (1.0 - sigmoid_v))).astype(jnp.bfloat16)
    grad_picked = jnp.einsum("gcj,ckj->gck", grad_pre, weights, preferred_element_type=jnp.float32)
    grad_picked = grad_picked.reshape(group_rows, col_blocks * per_block, emb_width)
    own_flat = own_pattern.reshape(-1)
    onehot = (own_flat[:, None] == jnp.arange(feat_count, dtype=jnp.int32)[None, :]).astype(
        jnp.float32
    )
    partial_value = jnp.einsum("gme,mf->gfe", grad_picked, onehot, precision=lax.Precision.HIGHEST)
    grad_pooled = lax.psum_scatter(
        partial_value.astype(jnp.bfloat16), "table", scatter_dimension=0, tiled=True
    ).astype(jnp.float32)
    spread = jnp.broadcast_to(
        grad_pooled[:, :, None, :], (samples, feat_count, bag_depth, emb_width)
    )
    spread = jnp.where(bag_live[..., None], spread, jnp.float32(0.0)).reshape(-1, emb_width)
    segment_ids = jnp.where(bag_live, bag_index, peer_count * slot_cap).reshape(-1)
    slot_grads = jax.ops.segment_sum(spread, segment_ids, num_segments=peer_count * slot_cap + 1)
    slot_grads = slot_grads[: peer_count * slot_cap].reshape(peer_count, slot_cap, emb_width)
    returned = lax.all_to_all(
        slot_grads.astype(jnp.bfloat16), "table", split_axis=0, concat_axis=0, tiled=True
    ).astype(slot_grads.dtype)
    row_ids = jnp.where(is_live, request_list, row_count).reshape(-1)
    row_grads = jax.ops.segment_sum(
        returned.reshape(-1, emb_width), row_ids, num_segments=row_count + 1
    )
    row_grads = row_grads[:row_count].reshape(1, row_count, emb_width)
    return (activation, row_grads)


def contract(lhs, rhs, lhs_dim, rhs_dim):
    return lax.dot_general(
        lhs, rhs, (((lhs_dim,), (rhs_dim,)), ((), ())), preferred_element_type=F32
    )


def body(
    n_table,
    n_fsdp,
    chunks,
    table_in,
    req_in,
    bag_in,
    pattern_in,
    tiles_ref,
    cot_ref,
    act_ref,
    rows_ref,
    table_ref,
    req_ref,
    bag_ref,
    pattern_ref,
    w,
    cot,
    act,
    req_row,
    bag_rows,
    pick,
    counts,
    received,
    values,
    spread,
    pooled,
    products,
    back,
    back_in,
    plan,
    plan_s,
    local_sem,
    load_sem,
    w_send,
    w_recv,
    t_send,
    t_recv,
):
    col_blocks, per_block, tile_rows, emb = tiles_ref.shape
    step = col_blocks // chunks
    lines = n_fsdp // 2
    samples, depth, feats = bag_ref.shape[1:]
    slot_cap = req_ref.shape[3]
    slots = n_table * slot_cap
    group = cot_ref.shape[1]
    row_count = table_ref.shape[1]
    pad = bag_rows.shape[3] // (samples // bag_rows.shape[1])

    me = lax.axis_index("table")
    mine = lax.axis_index("fsdp")
    z = mine // 2
    core = mine % 2
    sibling = 2 * z + 1 - core

    loads = [
        pltpu.make_async_copy(source, target, load_sem.at[i])
        for i, (source, target) in enumerate(
            (
                (req_in, req_ref),
                (table_in, table_ref),
                (bag_in, bag_ref),
                (pattern_in, pattern_ref),
            )
        )
    ]
    barrier = pltpu.get_barrier_semaphore()
    for d in range(1, n_table):
        pl.semaphore_signal(
            barrier, inc=1, device_id={"table": lax.rem(me + d, n_table)}, device_id_type=MESH
        )
    pl.semaphore_signal(barrier, inc=1, device_id={"fsdp": sibling}, device_id_type=MESH)

    @pl.when(z > 0)
    def _():
        pl.semaphore_signal(barrier, inc=1, device_id={"fsdp": mine - 2}, device_id_type=MESH)

    @pl.when(z < lines - 1)
    def _():
        pl.semaphore_signal(barrier, inc=1, device_id={"fsdp": mine + 2}, device_id_type=MESH)

    for load in loads:
        load.start()
    own_tiles = pltpu.make_async_copy(
        tiles_ref,
        w.at[:, :, pl.ds(pl.multiple_of(mine * tile_rows, tile_rows), tile_rows), :],
        local_sem.at[0],
    )
    own_cot = pltpu.make_async_copy(cot_ref.at[0], cot, local_sem.at[1])
    own_cot.start()

    neighbours = jnp.where(z > 0, 1, 0) + jnp.where(z < lines - 1, 1, 0)
    pl.semaphore_wait(barrier, n_table + neighbours)

    def slot(chunk, source):
        at = pl.multiple_of(source * tile_rows, tile_rows)
        return w.at[pl.ds(chunk * step, step), :, pl.ds(at, tile_rows), :]

    def hop(way, chunk, line, target, own=False):
        source = 2 * line + core
        src = tiles_ref.at[pl.ds(chunk * step, step)] if own else slot(chunk, source)
        return pltpu.make_async_remote_copy(
            src_ref=src,
            dst_ref=slot(chunk, source),
            send_sem=w_send.at[way, chunk, line],
            recv_sem=w_recv.at[chunk, source],
            device_id={"fsdp": target},
            device_id_type=MESH,
        )

    def landed(chunk, source):
        pltpu.make_async_remote_copy(
            src_ref=slot(chunk, source),
            dst_ref=slot(chunk, source),
            send_sem=w_send.at[2, chunk, z],
            recv_sem=w_recv.at[chunk, source],
            device_id={"fsdp": sibling},
            device_id_type=MESH,
        ).wait_recv()

    def send_own(chunk, carry):
        @pl.when(z < lines - 1)
        def _():
            hop(0, chunk, z, mine + 2, True).start()

        @pl.when(z > 0)
        def _():
            hop(1, chunk, z, mine - 2, True).start()

        return carry

    lax.fori_loop(0, chunks, send_own, 0)

    def send_own_core(chunk, carry):
        hop(2, chunk, z, sibling, True).start()
        return carry

    lax.fori_loop(0, chunks, send_own_core, 0)

    def exchange(phase, source_of, target):
        copies = []
        for d in range(1, n_table):
            peer = lax.rem(me + d, n_table)
            copy = pltpu.make_async_remote_copy(
                src_ref=source_of(peer),
                dst_ref=target,
                send_sem=t_send.at[phase, d],
                recv_sem=t_recv.at[phase, d],
                device_id={"table": peer},
                device_id_type=MESH,
            )
            copy.start()
            copies.append(copy)
        return copies

    own_tiles.start()
    loads[0].wait()
    for d in range(n_table):
        req_row[:, d * slot_cap : (d + 1) * slot_cap] = req_ref[0, 0, d : d + 1, :]
    row_ids = lax.broadcasted_iota(jnp.int32, (row_count, slots), 0)
    pick[...] = jnp.where(row_ids == req_row[...], 1.0, 0.0).astype(BF16)
    loads[1].wait()
    received[me] = (
        contract(pick[...], table_ref[0], 0, 0).astype(BF16).reshape(n_table, slot_cap, emb)
    )
    first = exchange(0, lambda peer: received.at[me], received.at[me])
    loads[2].wait()
    loads[3].wait()
    quads = bag_rows.shape[1]
    per_row = samples // quads
    width = per_row * pad
    bag_rows[me] = jnp.full(bag_rows.shape[1:], -1, jnp.int32)
    for s in range(samples):
        at = (s % per_row) * pad
        bag_rows[me, s // per_row, :, at : at + feats] = bag_ref[0, s]
    second = exchange(1, lambda peer: bag_rows.at[me], bag_rows.at[me])

    plan[...] = jnp.zeros(plan.shape, jnp.int32)
    feat_ids = lax.broadcasted_iota(jnp.int32, (plan.shape[0] - 8, pattern_ref.shape[1]), 0)
    inverse = jnp.full(feat_ids.shape, per_block, jnp.int32)
    for i in range(per_block):
        inverse = jnp.where(feat_ids == pattern_ref[i : i + 1, :], i, inverse)
    plan[0 : plan.shape[0] - 8, 0 : pattern_ref.shape[1]] = inverse
    plan[plan.shape[0] - 8 : plan.shape[0] - 8 + per_block, 0 : pattern_ref.shape[1]] = pattern_ref[
        ...
    ]
    to_scalar = pltpu.make_async_copy(plan, plan_s, local_sem.at[2])
    to_scalar.start()
    products[:, per_block] = jnp.zeros((step, group, emb), F32)
    spread[...] = jnp.zeros(spread.shape, F32)

    for copy in second:
        copy.wait_recv()
    slot_ids = lax.broadcasted_iota(jnp.int32, (slots, width), 0)

    def count(d, carry):
        for g in range(quads):
            rows = bag_rows[d, g]
            found = jnp.zeros((slots, width), F32)
            for k in range(depth):
                found = found + jnp.where(slot_ids == rows[k : k + 1, :], 1.0, 0.0)
            counts[d, :, g * width : (g + 1) * width] = found.astype(BF16)
        return carry

    lax.fori_loop(0, n_table, count, 0)
    for copy in first:
        copy.wait_recv()

    def pool(d, carry):
        rows = jnp.concatenate([received[o, d] for o in range(n_table)], axis=0)
        values[...] = contract(counts[d], rows, 0, 0)
        at = pl.ds(pl.multiple_of(d * samples, samples), samples)
        for j in range(feats):
            pooled[j, at, :] = values[pl.ds(j, samples, stride=pad), :].astype(BF16)
        return carry

    lax.fori_loop(0, n_table, pool, 0)
    to_scalar.wait()
    own_cot.wait()
    own_tiles.wait()

    def arrive(chunk, distance):
        @pl.when(z >= distance)
        def _():
            landed(chunk, mine - 2 * distance)

            @pl.when(z < lines - 1)
            def _():
                hop(0, chunk, z - distance, mine + 2).start()

            hop(2, chunk, z - distance, sibling).start()

        @pl.when(z + distance < lines)
        def _():
            landed(chunk, mine + 2 * distance)

            @pl.when(z > 0)
            def _():
                hop(1, chunk, z + distance, mine - 2).start()

            hop(2, chunk, z + distance, sibling).start()

    for distance in range(1, lines - 1):
        lax.fori_loop(
            0, chunks, lambda chunk, carry, distance=distance: (arrive(chunk, distance), carry)[1], 0
        )

    def work(chunk, carry):
        arrive(chunk, lines - 1)
        for line in range(lines):
            landed(chunk, 2 * line + 1 - core)
        blocks = [chunk * step + b for b in range(step)]
        weights = [w[n].reshape(per_block * emb, emb) for n in blocks]
        pres = []
        for b, n in enumerate(blocks):
            picked = jnp.concatenate(
                [
                    pooled[plan_s[plan.shape[0] - 8 + i, me * col_blocks + n]]
                    for i in range(per_block)
                ],
                axis=1,
            )
            pres.append(contract(picked, weights[b], 1, 0))
        grads = []
        for n, pre in zip(blocks, pres):
            sig = jax.nn.sigmoid(pre)
            columns = pl.ds(pl.multiple_of(n * emb, emb), emb)
            act[:, columns] = (pre * sig).astype(BF16)
            up = cot[:, columns].astype(F32)
            grads.append((up * sig * (1.0 + pre * (1.0 - sig))).astype(BF16))
        for b in range(step):
            back_rows = contract(grads[b], weights[b], 1, 1)
            for i in range(per_block):
                products[b, i] = back_rows[:, i * emb : (i + 1) * emb]

        def add(j, c):
            value = products[0, plan_s[j, me * col_blocks + chunk * step]]
            for b in range(1, step):
                value = value + products[b, plan_s[j, me * col_blocks + chunk * step + b]]
            at = pl.ds(j, group, stride=pad)
            spread[at, :] = spread[at, :] + value
            return c

        lax.fori_loop(0, feats, add, 0, unroll=2)
        return carry

    lax.fori_loop(0, chunks, work, 0)
    act_out = pltpu.make_async_copy(act, act_ref.at[0], local_sem.at[3])
    act_out.start()

    partial = spread[...].astype(BF16)
    for d in range(n_table):
        rows = partial[d * samples * pad : (d + 1) * samples * pad]
        slot_grads = contract(counts[d], rows, 1, 0).astype(BF16)
        for o in range(n_table):
            back[o, d] = slot_grads[o * slot_cap : (o + 1) * slot_cap]
    third = exchange(2, lambda peer: back.at[peer], back_in.at[me])
    back_in[me] = back[me]
    for copy in third:
        copy.wait_recv()
    summed = back_in[0].astype(F32)
    for t in range(1, n_table):
        summed = summed + back_in[t].astype(F32)
    summed = summed.reshape(slots, emb)
    high = summed.astype(BF16)
    low = (summed - high.astype(F32)).astype(BF16)
    rows_ref[0] = contract(pick[...], high, 1, 0) + contract(pick[...], low, 1, 0)

    for copies in (first, second, third):
        for copy in copies:
            copy.wait_send()

    def sent_all(chunk, carry):
        for line in range(lines):
            hop(2, chunk, line, sibling).wait_send()

            @pl.when((line <= z) & (z < lines - 1))
            def _():
                hop(0, chunk, line, mine + 2).wait_send()

            @pl.when((line >= z) & (z > 0))
            def _():
                hop(1, chunk, line, mine - 2).wait_send()

        return carry

    lax.fori_loop(0, chunks, sent_all, 0)
    act_out.wait()


def fused(n_table, n_fsdp, chunks, table_rows, requests, bag_slots, pattern, tiles, cotangent):
    col_blocks, per_block, tile_rows, emb = tiles.shape
    group = cotangent.shape[1]
    row_count = table_rows.shape[1]
    samples, feats, depth = bag_slots.shape[1:]
    slot_cap = requests.shape[3]
    slots = n_table * slot_cap
    lines = n_fsdp // 2
    pad = 32
    per_row = 128 // pad
    plan_rows = pad + 8
    vmem, anywhere = pl.BlockSpec(memory_space=pltpu.VMEM), pl.BlockSpec(memory_space=pl.ANY)
    hbm = pl.BlockSpec(memory_space=pltpu.HBM)
    bags = jnp.swapaxes(bag_slots, 2, 3)
    return pl.pallas_call(
        functools.partial(body, n_table, n_fsdp, chunks),
        out_shape=(
            jax.ShapeDtypeStruct((1, group, col_blocks * emb), BF16),
            jax.ShapeDtypeStruct((1, row_count, emb), F32),
        ),
        in_specs=[hbm] * 6,
        out_specs=(anywhere, vmem),
        scratch_shapes=[
            pltpu.VMEM(table_rows.shape, BF16),
            pltpu.VMEM(requests.shape, jnp.int32),
            pltpu.VMEM(bags.shape, jnp.int32),
            pltpu.VMEM(pattern.shape[::-1], jnp.int32),
            pltpu.VMEM((col_blocks, per_block, tile_rows * n_fsdp, emb), BF16),
            pltpu.VMEM((group, col_blocks * emb), BF16),
            pltpu.VMEM((group, col_blocks * emb), BF16),
            pltpu.VMEM((1, slots), jnp.int32),
            pltpu.VMEM((n_table, samples // per_row, depth, per_row * pad), jnp.int32),
            pltpu.VMEM((row_count, slots), BF16),
            pltpu.VMEM((n_table, slots, samples * pad), BF16),
            pltpu.VMEM((n_table, n_table, slot_cap, emb), BF16),
            pltpu.VMEM((samples * pad, emb), F32),
            pltpu.VMEM((group * pad, emb), F32),
            pltpu.VMEM((feats, group, emb), BF16),
            pltpu.VMEM((col_blocks // chunks, per_block + 1, group, emb), F32),
            pltpu.VMEM((n_table, n_table, slot_cap, emb), BF16),
            pltpu.VMEM((n_table, n_table, slot_cap, emb), BF16),
            pltpu.VMEM((plan_rows, 128), jnp.int32),
            pltpu.SMEM((plan_rows, 128), jnp.int32),
            pltpu.SemaphoreType.DMA((4,)),
            pltpu.SemaphoreType.DMA((4,)),
            pltpu.SemaphoreType.DMA((3, chunks, lines)),
            pltpu.SemaphoreType.DMA((chunks, n_fsdp)),
            pltpu.SemaphoreType.DMA((3, n_table)),
            pltpu.SemaphoreType.DMA((3, n_table)),
        ],
        compiler_params=pltpu.CompilerParams(
            collective_id=0, has_side_effects=True, vmem_limit_bytes=VMEM_LIMIT
        ),
    )(
        table_rows,
        requests,
        bags,
        pattern.T,
        tiles,
        cotangent,
    )


def solution(mesh):
    n_table, n_fsdp = mesh.shape["table"], mesh.shape["fsdp"]
    in_specs = (
        P("fsdp", "table", None),
        P("fsdp", "table", None, None),
        P("fsdp", "table", None, None),
        P(),
        P("table", None, "fsdp", None),
        P("fsdp", None, "table"),
    )
    out_specs = (P("fsdp", None, "table"), P("fsdp", "table", None))

    def program(table_rows, requests, bag_slots, pattern, tiles, cotangent):
        col_blocks, _, tile_rows, emb = tiles.shape
        samples, feats = bag_slots.shape[1:3]
        whole = (
            tile_rows % TILE_ROWS == 0
            and samples % TILE_ROWS == 0
            and emb == 128
            and n_table * requests.shape[3] == 128
            and feats <= 32
            and n_fsdp % 2 == 0
            and col_blocks % CHUNKS == 0
        )
        if whole:
            run = functools.partial(fused, n_table, n_fsdp, CHUNKS)
        else:
            run = local
        return run(table_rows, requests, bag_slots, pattern, tiles, cotangent)

    return jax.shard_map(program, mesh=mesh, in_specs=in_specs, out_specs=out_specs, check_vma=False)
```

```python
import functools

import jax
import jax.numpy as jnp
from jax import lax
from jax.experimental import pallas as pl
from jax.experimental.pallas import tpu as pltpu
from jax.sharding import PartitionSpec as P

MESH = pl.DeviceIdType.MESH
F32 = jnp.float32
BF16 = jnp.bfloat16
TILE_ROWS = 16
VMEM_LIMIT = 64 * 1024 * 1024
CUTS = (0, 0.5, 1)


def local(table_rows, requests, bag_slots, pattern, tiles, cotangent):
    table_shard = table_rows[0]
    row_count = table_shard.shape[0]
    emb_width = table_shard.shape[1]
    request_list = requests[0, 0]
    peer_count = request_list.shape[0]
    slot_cap = request_list.shape[1]
    is_live = request_list >= 0
    sent_rows = jnp.take(table_shard, jnp.where(is_live, request_list, 0), axis=0)
    sent_rows = jnp.where(is_live[..., None], sent_rows, jnp.zeros_like(sent_rows))
    received = lax.all_to_all(sent_rows, "table", split_axis=0, concat_axis=0, tiled=True)
    slot_rows = received.reshape(peer_count * slot_cap, emb_width)
    bag_index = bag_slots[0]
    samples = bag_index.shape[0]
    feat_count = bag_index.shape[1]
    bag_depth = bag_index.shape[2]
    bag_live = bag_index >= 0
    values = jnp.take(slot_rows, jnp.where(bag_live, bag_index, 0).reshape(-1), axis=0)
    values = values.reshape(samples, feat_count, bag_depth, emb_width).astype(jnp.float32)
    values = jnp.where(bag_live[..., None], values, jnp.float32(0.0))
    pooled = jnp.sum(values, axis=2).astype(jnp.bfloat16)
    col_blocks = tiles.shape[0]
    per_block = tiles.shape[1]
    my_index = lax.axis_index("table")
    own_pattern = lax.dynamic_slice_in_dim(pattern, my_index * col_blocks, col_blocks, 0)
    group_rows = cotangent.shape[1]
    gathered = lax.all_gather(pooled, "table", axis=0, tiled=True)
    picked = jnp.take(gathered, own_pattern.reshape(-1), axis=1)
    picked = picked.reshape(group_rows, col_blocks, per_block * emb_width)
    full_tiles = lax.all_gather(tiles, "fsdp", axis=2, tiled=True)
    weights = full_tiles.reshape(col_blocks, per_block * emb_width, emb_width)
    pre_act = jnp.einsum("gck,ckj->gcj", picked, weights, preferred_element_type=jnp.float32)
    activation = (
        jax.nn.silu(pre_act).astype(jnp.bfloat16).reshape(1, group_rows, col_blocks * emb_width)
    )
    sigmoid_v = jax.nn.sigmoid(pre_act)
    upstream = cotangent[0].reshape(group_rows, col_blocks, emb_width).astype(jnp.float32)
    grad_pre = (upstream * sigmoid_v * (1.0 + pre_act * (1.0 - sigmoid_v))).astype(jnp.bfloat16)
    grad_picked = jnp.einsum("gcj,ckj->gck", grad_pre, weights, preferred_element_type=jnp.float32)
    grad_picked = grad_picked.reshape(group_rows, col_blocks * per_block, emb_width)
    own_flat = own_pattern.reshape(-1)
    onehot = (own_flat[:, None] == jnp.arange(feat_count, dtype=jnp.int32)[None, :]).astype(
        jnp.float32
    )
    partial_value = jnp.einsum("gme,mf->gfe", grad_picked, onehot, precision=lax.Precision.HIGHEST)
    grad_pooled = lax.psum_scatter(
        partial_value.astype(jnp.bfloat16), "table", scatter_dimension=0, tiled=True
    ).astype(jnp.float32)
    spread = jnp.broadcast_to(
        grad_pooled[:, :, None, :], (samples, feat_count, bag_depth, emb_width)
    )
    spread = jnp.where(bag_live[..., None], spread, jnp.float32(0.0)).reshape(-1, emb_width)
    segment_ids = jnp.where(bag_live, bag_index, peer_count * slot_cap).reshape(-1)
    slot_grads = jax.ops.segment_sum(spread, segment_ids, num_segments=peer_count * slot_cap + 1)
    slot_grads = slot_grads[: peer_count * slot_cap].reshape(peer_count, slot_cap, emb_width)
    returned = lax.all_to_all(
        slot_grads.astype(jnp.bfloat16), "table", split_axis=0, concat_axis=0, tiled=True
    ).astype(slot_grads.dtype)
    row_ids = jnp.where(is_live, request_list, row_count).reshape(-1)
    row_grads = jax.ops.segment_sum(
        returned.reshape(-1, emb_width), row_ids, num_segments=row_count + 1
    )
    row_grads = row_grads[:row_count].reshape(1, row_count, emb_width)
    return (activation, row_grads)


def contract(lhs, rhs, lhs_dim, rhs_dim):
    return lax.dot_general(
        lhs, rhs, (((lhs_dim,), (rhs_dim,)), ((), ())), preferred_element_type=F32
    )


def body(
    n_table,
    n_fsdp,
    starts,
    table_in,
    req_in,
    bag_in,
    pattern_in,
    tiles_ref,
    cot_ref,
    act_ref,
    rows_ref,
    table_ref,
    req_ref,
    bag_ref,
    pattern_ref,
    w,
    cot,
    act,
    req_row,
    bag_rows,
    bag_slots,
    pick,
    counts,
    received,
    total,
    pooled,
    products,
    back,
    back_in,
    plan,
    plan_s,
    local_sem,
    load_sem,
    w_send,
    w_recv,
    t_send,
    t_recv,
):
    col_blocks, per_block, tile_rows, emb = tiles_ref.shape
    chunks = len(starts) - 1
    lines = n_fsdp // 2
    samples, depth, feats = bag_ref.shape[1:]
    slot_cap = req_ref.shape[3]
    slots = n_table * slot_cap
    group = cot_ref.shape[1]
    row_count = table_ref.shape[1]
    pad = bag_rows.shape[2] // (samples // bag_rows.shape[0])

    me = lax.axis_index("table")
    mine = lax.axis_index("fsdp")
    z = mine // 2
    core = mine % 2
    sibling = 2 * z + 1 - core

    loads = [
        pltpu.make_async_copy(source, target, load_sem.at[i])
        for i, (source, target) in enumerate(
            (
                (req_in, req_ref),
                (table_in, table_ref),
                (bag_in, bag_ref),
                (pattern_in, pattern_ref),
            )
        )
    ]
    barrier = pltpu.get_barrier_semaphore()
    for d in range(1, n_table):
        pl.semaphore_signal(
            barrier, inc=1, device_id={"table": lax.rem(me + d, n_table)}, device_id_type=MESH
        )
    pl.semaphore_signal(barrier, inc=1, device_id={"fsdp": sibling}, device_id_type=MESH)

    @pl.when(z > 0)
    def _():
        pl.semaphore_signal(barrier, inc=1, device_id={"fsdp": mine - 2}, device_id_type=MESH)

    @pl.when(z < lines - 1)
    def _():
        pl.semaphore_signal(barrier, inc=1, device_id={"fsdp": mine + 2}, device_id_type=MESH)

    for load in loads:
        load.start()
    own_tiles = pltpu.make_async_copy(
        tiles_ref,
        w.at[:, :, pl.ds(pl.multiple_of(mine * tile_rows, tile_rows), tile_rows), :],
        local_sem.at[0],
    )
    own_cot = pltpu.make_async_copy(cot_ref.at[0], cot, local_sem.at[1])
    own_cot.start()

    neighbours = jnp.where(z > 0, 1, 0) + jnp.where(z < lines - 1, 1, 0)
    pl.semaphore_wait(barrier, n_table + neighbours)

    def slot(chunk, source):
        at = pl.multiple_of(source * tile_rows, tile_rows)
        return w.at[starts[chunk] : starts[chunk + 1], :, pl.ds(at, tile_rows), :]

    def hop(way, chunk, line, target, own=False):
        source = 2 * line + core
        src = tiles_ref.at[starts[chunk] : starts[chunk + 1]] if own else slot(chunk, source)
        return pltpu.make_async_remote_copy(
            src_ref=src,
            dst_ref=slot(chunk, source),
            send_sem=w_send.at[way, chunk, line],
            recv_sem=w_recv.at[chunk, source],
            device_id={"fsdp": target},
            device_id_type=MESH,
        )

    def landed(chunk, source):
        pltpu.make_async_remote_copy(
            src_ref=slot(chunk, source),
            dst_ref=slot(chunk, source),
            send_sem=w_send.at[2, chunk, z],
            recv_sem=w_recv.at[chunk, source],
            device_id={"fsdp": sibling},
            device_id_type=MESH,
        ).wait_recv()

    def send_own(chunk, carry):
        @pl.when(z < lines - 1)
        def _():
            hop(0, chunk, z, mine + 2, True).start()

        @pl.when(z > 0)
        def _():
            hop(1, chunk, z, mine - 2, True).start()

        return carry

    for chunk in range(chunks):
        send_own(chunk, 0)

    def send_own_core(chunk, carry):
        hop(2, chunk, z, sibling, True).start()
        return carry

    for chunk in range(chunks):
        send_own_core(chunk, 0)

    def exchange(phase, source_of, target):
        copies = []
        for d in range(1, n_table):
            peer = lax.rem(me + d, n_table)
            copy = pltpu.make_async_remote_copy(
                src_ref=source_of(peer),
                dst_ref=target,
                send_sem=t_send.at[phase, d],
                recv_sem=t_recv.at[phase, d],
                device_id={"table": peer},
                device_id_type=MESH,
            )
            copy.start()
            copies.append(copy)
        return copies

    own_tiles.start()
    loads[0].wait()
    for d in range(n_table):
        req_row[:, d * slot_cap : (d + 1) * slot_cap] = req_ref[0, 0, d : d + 1, :]
    row_ids = lax.broadcasted_iota(jnp.int32, (row_count, slots), 0)
    pick[...] = jnp.where(row_ids == req_row[...], 1.0, 0.0).astype(BF16)
    loads[1].wait()
    received[me] = (
        contract(pick[...], table_ref[0], 0, 0).astype(BF16).reshape(n_table, slot_cap, emb)
    )
    first = exchange(0, lambda peer: received.at[me], received.at[me])
    loads[2].wait()
    loads[3].wait()
    quads = bag_rows.shape[0]
    per_row = samples // quads
    width = per_row * pad
    bag_rows[...] = jnp.full(bag_rows.shape, -1, jnp.int32)
    for s in range(samples):
        at = (s % per_row) * pad
        bag_rows[s // per_row, 0:depth, at : at + feats] = bag_ref[0, s]
    by_sample = jnp.concatenate([bag_rows[g] for g in range(quads)], axis=1)
    total_width = quads * width
    source = lax.broadcasted_iota(jnp.int32, (total_width, total_width), 0)
    target = lax.broadcasted_iota(jnp.int32, (total_width, total_width), 1)
    moves = (target % samples) * pad + target // samples == source
    by_feature = contract(
        by_sample.astype(F32).astype(BF16), jnp.where(moves, 1.0, 0.0).astype(BF16), 1, 0
    )
    used = lax.broadcasted_iota(jnp.int32, by_feature.shape, 1) < feats * samples
    bag_slots[me] = jnp.where(used, by_feature, -1.0)
    second = exchange(1, lambda peer: bag_slots.at[me], bag_slots.at[me])

    plan[...] = jnp.zeros(plan.shape, jnp.int32)
    feat_ids = lax.broadcasted_iota(jnp.int32, (plan.shape[0] - 8, pattern_ref.shape[1]), 0)
    inverse = jnp.full(feat_ids.shape, per_block, jnp.int32)
    for i in range(per_block):
        inverse = jnp.where(feat_ids == pattern_ref[i : i + 1, :], i, inverse)
    plan[0 : plan.shape[0] - 8, 0 : pattern_ref.shape[1]] = inverse
    plan[plan.shape[0] - 8 : plan.shape[0] - 8 + per_block, 0 : pattern_ref.shape[1]] = pattern_ref[
        ...
    ]
    to_scalar = pltpu.make_async_copy(plan, plan_s, local_sem.at[2])
    to_scalar.start()
    products[:, per_block] = jnp.zeros((products.shape[0], group, emb), F32)
    total[...] = jnp.zeros(total.shape, F32)

    for copy in second:
        copy.wait_recv()
    slot_ids = lax.broadcasted_iota(jnp.int32, (slots, width), 0).astype(F32)

    def count(d, carry):
        for g in range(quads):
            rows = bag_slots[d, :, g * width : (g + 1) * width]
            found = jnp.zeros((slots, width), F32)
            for k in range(depth):
                found = found + jnp.where(slot_ids == rows[k : k + 1, :], 1.0, 0.0)
            counts[d, :, g * width : (g + 1) * width] = found.astype(BF16)
        return carry

    lax.fori_loop(0, n_table, count, 0)
    for copy in first:
        copy.wait_recv()

    def pool(d, carry):
        rows = jnp.concatenate([received[o, d] for o in range(n_table)], axis=0)
        values = contract(counts[d], rows, 0, 0).astype(BF16)
        at = pl.ds(pl.multiple_of(d * samples, samples), samples)
        pooled[:, at, :] = values[: feats * samples].reshape(feats, samples, emb)
        return carry

    lax.fori_loop(0, n_table, pool, 0)
    to_scalar.wait()
    own_cot.wait()
    own_tiles.wait()

    def arrive(chunk, distance):
        @pl.when(z >= distance)
        def _():
            landed(chunk, mine - 2 * distance)

            @pl.when(z < lines - 1)
            def _():
                hop(0, chunk, z - distance, mine + 2).start()

            hop(2, chunk, z - distance, sibling).start()

        @pl.when(z + distance < lines)
        def _():
            landed(chunk, mine + 2 * distance)

            @pl.when(z > 0)
            def _():
                hop(1, chunk, z + distance, mine - 2).start()

            hop(2, chunk, z + distance, sibling).start()

    for distance in range(1, lines - 1):
        for chunk in range(chunks):
            arrive(chunk, distance)

    def work(chunk, carry):
        arrive(chunk, lines - 1)
        for line in range(lines):
            landed(chunk, 2 * line + 1 - core)
        blocks = range(starts[chunk], starts[chunk + 1])
        step = len(blocks)
        weights = [w[n].reshape(per_block * emb, emb) for n in blocks]
        pres = []
        for b, n in enumerate(blocks):
            picked = jnp.concatenate(
                [
                    pooled[plan_s[plan.shape[0] - 8 + i, me * col_blocks + n]]
                    for i in range(per_block)
                ],
                axis=1,
            )
            pres.append(contract(picked, weights[b], 1, 0))
        grads = []
        for n, pre in zip(blocks, pres):
            sig = jax.nn.sigmoid(pre)
            columns = slice(n * emb, (n + 1) * emb)
            act[:, columns] = (pre * sig).astype(BF16)
            up = cot[:, columns].astype(F32)
            grads.append((up * sig * (1.0 + pre * (1.0 - sig))).astype(BF16))
        for b in range(step):
            back_rows = contract(grads[b], weights[b], 1, 1)
            for i in range(per_block):
                products[b, i] = back_rows[:, i * emb : (i + 1) * emb]

        def add(j, c):
            value = products[0, plan_s[j, me * col_blocks + blocks[0]]]
            for b in range(1, step):
                value = value + products[b, plan_s[j, me * col_blocks + blocks[b]]]
            total[j] = total[j] + value
            return c

        lax.fori_loop(0, feats, add, 0, unroll=True)
        return carry

    for chunk in range(chunks):
        work(chunk, 0)
    act_out = pltpu.make_async_copy(act, act_ref.at[0], local_sem.at[3])
    act_out.start()

    for d in range(n_table):
        rows = total[:, d * samples : (d + 1) * samples, :].astype(BF16)
        rows = rows.reshape(feats * samples, emb)
        slot_grads = contract(counts[d, :, 0 : feats * samples], rows, 1, 0).astype(BF16)
        for o in range(n_table):
            back[o, d] = slot_grads[o * slot_cap : (o + 1) * slot_cap]
    third = exchange(2, lambda peer: back.at[peer], back_in.at[me])
    back_in[me] = back[me]
    for copy in third:
        copy.wait_recv()
    summed = back_in[0].astype(F32)
    for t in range(1, n_table):
        summed = summed + back_in[t].astype(F32)
    summed = summed.reshape(slots, emb)
    high = summed.astype(BF16)
    low = (summed - high.astype(F32)).astype(BF16)
    rows_ref[0] = contract(pick[...], high, 1, 0) + contract(pick[...], low, 1, 0)

    for copies in (first, second, third):
        for copy in copies:
            copy.wait_send()

    def sent_all(chunk, carry):
        for line in range(lines):
            hop(2, chunk, line, sibling).wait_send()

            @pl.when((line <= z) & (z < lines - 1))
            def _():
                hop(0, chunk, line, mine + 2).wait_send()

            @pl.when((line >= z) & (z > 0))
            def _():
                hop(1, chunk, line, mine - 2).wait_send()

        return carry

    for chunk in range(chunks):
        sent_all(chunk, 0)
    act_out.wait()


def fused(n_table, n_fsdp, table_rows, requests, bag_slots, pattern, tiles, cotangent):
    col_blocks, per_block, tile_rows, emb = tiles.shape
    group = cotangent.shape[1]
    row_count = table_rows.shape[1]
    samples, feats, depth = bag_slots.shape[1:]
    slot_cap = requests.shape[3]
    slots = n_table * slot_cap
    lines = n_fsdp // 2
    starts = tuple(round(col_blocks * cut) for cut in CUTS)
    longest = max(b - a for a, b in zip(starts, starts[1:]))
    chunks = len(starts) - 1
    pad = 32
    per_row = 128 // pad
    plan_rows = pad + 8
    vmem, anywhere = pl.BlockSpec(memory_space=pltpu.VMEM), pl.BlockSpec(memory_space=pl.ANY)
    hbm = pl.BlockSpec(memory_space=pltpu.HBM)
    bags = jnp.swapaxes(bag_slots, 2, 3)
    return pl.pallas_call(
        functools.partial(body, n_table, n_fsdp, starts),
        out_shape=(
            jax.ShapeDtypeStruct((1, group, col_blocks * emb), BF16),
            jax.ShapeDtypeStruct((1, row_count, emb), F32),
        ),
        in_specs=[hbm] * 6,
        out_specs=(anywhere, vmem),
        scratch_shapes=[
            pltpu.VMEM(table_rows.shape, BF16),
            pltpu.VMEM(requests.shape, jnp.int32),
            pltpu.VMEM(bags.shape, jnp.int32),
            pltpu.VMEM(pattern.shape[::-1], jnp.int32),
            pltpu.VMEM((col_blocks, per_block, tile_rows * n_fsdp, emb), BF16),
            pltpu.VMEM((group, col_blocks * emb), BF16),
            pltpu.VMEM((group, col_blocks * emb), BF16),
            pltpu.VMEM((1, slots), jnp.int32),
            pltpu.VMEM((samples // per_row, 8, per_row * pad), jnp.int32),
            pltpu.VMEM((n_table, 8, samples * pad), F32),
            pltpu.VMEM((row_count, slots), BF16),
            pltpu.VMEM((n_table, slots, samples * pad), BF16),
            pltpu.VMEM((n_table, n_table, slot_cap, emb), BF16),
            pltpu.VMEM((feats, group, emb), F32),
            pltpu.VMEM((feats, group, emb), BF16),
            pltpu.VMEM((longest, per_block + 1, group, emb), F32),
            pltpu.VMEM((n_table, n_table, slot_cap, emb), BF16),
            pltpu.VMEM((n_table, n_table, slot_cap, emb), BF16),
            pltpu.VMEM((plan_rows, 128), jnp.int32),
            pltpu.SMEM((plan_rows, 128), jnp.int32),
            pltpu.SemaphoreType.DMA((4,)),
            pltpu.SemaphoreType.DMA((4,)),
            pltpu.SemaphoreType.DMA((3, chunks, lines)),
            pltpu.SemaphoreType.DMA((chunks, n_fsdp)),
            pltpu.SemaphoreType.DMA((3, n_table)),
            pltpu.SemaphoreType.DMA((3, n_table)),
        ],
        compiler_params=pltpu.CompilerParams(
            collective_id=0, has_side_effects=True, vmem_limit_bytes=VMEM_LIMIT
        ),
    )(
        table_rows,
        requests,
        bags,
        pattern.T,
        tiles,
        cotangent,
    )


def solution(mesh):
    n_table, n_fsdp = mesh.shape["table"], mesh.shape["fsdp"]
    in_specs = (
        P("fsdp", "table", None),
        P("fsdp", "table", None, None),
        P("fsdp", "table", None, None),
        P(),
        P("table", None, "fsdp", None),
        P("fsdp", None, "table"),
    )
    out_specs = (P("fsdp", None, "table"), P("fsdp", "table", None))

    def program(table_rows, requests, bag_slots, pattern, tiles, cotangent):
        col_blocks, _, tile_rows, emb = tiles.shape
        samples, feats = bag_slots.shape[1:3]
        whole = (
            tile_rows % TILE_ROWS == 0
            and samples % TILE_ROWS == 0
            and emb == 128
            and n_table * requests.shape[3] == 128
            and feats <= 32
            and bag_slots.shape[3] <= 8
            and n_fsdp % 2 == 0
            and col_blocks % 16 == 0
        )
        if whole:
            run = functools.partial(fused, n_table, n_fsdp)
        else:
            run = local
        return run(table_rows, requests, bag_slots, pattern, tiles, cotangent)

    return jax.shard_map(program, mesh=mesh, in_specs=in_specs, out_specs=out_specs, check_vma=False)
```

```python
import functools

import jax
import jax.numpy as jnp
from jax import lax
from jax.experimental import pallas as pl
from jax.experimental.pallas import tpu as pltpu
from jax.sharding import PartitionSpec as P

MESH = pl.DeviceIdType.MESH
F32 = jnp.float32
BF16 = jnp.bfloat16
TILE_ROWS = 16
VMEM_LIMIT = 64 * 1024 * 1024
CUTS = (0, 0.5, 1)


def local(table_rows, requests, bag_slots, pattern, tiles, cotangent):
    table_shard = table_rows[0]
    row_count = table_shard.shape[0]
    emb_width = table_shard.shape[1]
    request_list = requests[0, 0]
    peer_count = request_list.shape[0]
    slot_cap = request_list.shape[1]
    is_live = request_list >= 0
    sent_rows = jnp.take(table_shard, jnp.where(is_live, request_list, 0), axis=0)
    sent_rows = jnp.where(is_live[..., None], sent_rows, jnp.zeros_like(sent_rows))
    received = lax.all_to_all(sent_rows, "table", split_axis=0, concat_axis=0, tiled=True)
    slot_rows = received.reshape(peer_count * slot_cap, emb_width)
    bag_index = bag_slots[0]
    samples = bag_index.shape[0]
    feat_count = bag_index.shape[1]
    bag_depth = bag_index.shape[2]
    bag_live = bag_index >= 0
    values = jnp.take(slot_rows, jnp.where(bag_live, bag_index, 0).reshape(-1), axis=0)
    values = values.reshape(samples, feat_count, bag_depth, emb_width).astype(jnp.float32)
    values = jnp.where(bag_live[..., None], values, jnp.float32(0.0))
    pooled = jnp.sum(values, axis=2).astype(jnp.bfloat16)
    col_blocks = tiles.shape[0]
    per_block = tiles.shape[1]
    my_index = lax.axis_index("table")
    own_pattern = lax.dynamic_slice_in_dim(pattern, my_index * col_blocks, col_blocks, 0)
    group_rows = cotangent.shape[1]
    gathered = lax.all_gather(pooled, "table", axis=0, tiled=True)
    picked = jnp.take(gathered, own_pattern.reshape(-1), axis=1)
    picked = picked.reshape(group_rows, col_blocks, per_block * emb_width)
    full_tiles = lax.all_gather(tiles, "fsdp", axis=2, tiled=True)
    weights = full_tiles.reshape(col_blocks, per_block * emb_width, emb_width)
    pre_act = jnp.einsum("gck,ckj->gcj", picked, weights, preferred_element_type=jnp.float32)
    activation = (
        jax.nn.silu(pre_act).astype(jnp.bfloat16).reshape(1, group_rows, col_blocks * emb_width)
    )
    sigmoid_v = jax.nn.sigmoid(pre_act)
    upstream = cotangent[0].reshape(group_rows, col_blocks, emb_width).astype(jnp.float32)
    grad_pre = (upstream * sigmoid_v * (1.0 + pre_act * (1.0 - sigmoid_v))).astype(jnp.bfloat16)
    grad_picked = jnp.einsum("gcj,ckj->gck", grad_pre, weights, preferred_element_type=jnp.float32)
    grad_picked = grad_picked.reshape(group_rows, col_blocks * per_block, emb_width)
    own_flat = own_pattern.reshape(-1)
    onehot = (own_flat[:, None] == jnp.arange(feat_count, dtype=jnp.int32)[None, :]).astype(
        jnp.float32
    )
    partial_value = jnp.einsum("gme,mf->gfe", grad_picked, onehot, precision=lax.Precision.HIGHEST)
    grad_pooled = lax.psum_scatter(
        partial_value.astype(jnp.bfloat16), "table", scatter_dimension=0, tiled=True
    ).astype(jnp.float32)
    spread = jnp.broadcast_to(
        grad_pooled[:, :, None, :], (samples, feat_count, bag_depth, emb_width)
    )
    spread = jnp.where(bag_live[..., None], spread, jnp.float32(0.0)).reshape(-1, emb_width)
    segment_ids = jnp.where(bag_live, bag_index, peer_count * slot_cap).reshape(-1)
    slot_grads = jax.ops.segment_sum(spread, segment_ids, num_segments=peer_count * slot_cap + 1)
    slot_grads = slot_grads[: peer_count * slot_cap].reshape(peer_count, slot_cap, emb_width)
    returned = lax.all_to_all(
        slot_grads.astype(jnp.bfloat16), "table", split_axis=0, concat_axis=0, tiled=True
    ).astype(slot_grads.dtype)
    row_ids = jnp.where(is_live, request_list, row_count).reshape(-1)
    row_grads = jax.ops.segment_sum(
        returned.reshape(-1, emb_width), row_ids, num_segments=row_count + 1
    )
    row_grads = row_grads[:row_count].reshape(1, row_count, emb_width)
    return (activation, row_grads)


def contract(lhs, rhs, lhs_dim, rhs_dim):
    return lax.dot_general(
        lhs, rhs, (((lhs_dim,), (rhs_dim,)), ((), ())), preferred_element_type=F32
    )


def body(
    n_table,
    n_fsdp,
    starts,
    table_in,
    req_in,
    bag_in,
    pattern_in,
    tiles_ref,
    cot_ref,
    act_ref,
    rows_ref,
    table_ref,
    req_ref,
    bag_ref,
    pattern_ref,
    w,
    cot,
    act,
    req_row,
    bag_rows,
    bag_slots,
    pick,
    counts,
    received,
    total,
    pooled,
    products,
    back,
    back_in,
    plan,
    plan_s,
    local_sem,
    load_sem,
    w_send,
    w_recv,
    t_send,
    t_recv,
):
    col_blocks, per_block, tile_rows, emb = tiles_ref.shape
    chunks = len(starts) - 1
    lines = n_fsdp // 2
    samples, depth, feats = bag_ref.shape[1:]
    slot_cap = req_ref.shape[3]
    slots = n_table * slot_cap
    group = cot_ref.shape[1]
    row_count = table_ref.shape[1]
    pad = bag_rows.shape[2] // (samples // bag_rows.shape[0])

    me = lax.axis_index("table")
    mine = lax.axis_index("fsdp")
    z = mine // 2
    core = mine % 2
    sibling = 2 * z + 1 - core

    loads = [
        pltpu.make_async_copy(source, target, load_sem.at[i])
        for i, (source, target) in enumerate(
            (
                (req_in, req_ref),
                (table_in, table_ref),
                (bag_in, bag_ref),
                (pattern_in, pattern_ref),
            )
        )
    ]
    barrier = pltpu.get_barrier_semaphore()
    for d in range(1, n_table):
        pl.semaphore_signal(
            barrier, inc=1, device_id={"table": lax.rem(me + d, n_table)}, device_id_type=MESH
        )
    pl.semaphore_signal(barrier, inc=1, device_id={"fsdp": sibling}, device_id_type=MESH)

    @pl.when(z > 0)
    def _():
        pl.semaphore_signal(barrier, inc=1, device_id={"fsdp": mine - 2}, device_id_type=MESH)

    @pl.when(z < lines - 1)
    def _():
        pl.semaphore_signal(barrier, inc=1, device_id={"fsdp": mine + 2}, device_id_type=MESH)

    for load in loads:
        load.start()
    own_tiles = pltpu.make_async_copy(
        tiles_ref,
        w.at[:, :, pl.ds(pl.multiple_of(mine * tile_rows, tile_rows), tile_rows), :],
        local_sem.at[0],
    )
    own_cot = pltpu.make_async_copy(cot_ref.at[0], cot, local_sem.at[1])
    own_tiles.start()
    own_cot.start()

    own_tiles.wait()
    neighbours = jnp.where(z > 0, 1, 0) + jnp.where(z < lines - 1, 1, 0)
    pl.semaphore_wait(barrier, n_table + neighbours)

    def slot(chunk, source):
        at = pl.multiple_of(source * tile_rows, tile_rows)
        return w.at[starts[chunk] : starts[chunk + 1], :, pl.ds(at, tile_rows), :]

    def hop(way, chunk, line, target, own=False):
        source = 2 * line + core
        src = slot(chunk, source)
        return pltpu.make_async_remote_copy(
            src_ref=src,
            dst_ref=slot(chunk, source),
            send_sem=w_send.at[way, chunk, line],
            recv_sem=w_recv.at[chunk, source],
            device_id={"fsdp": target},
            device_id_type=MESH,
        )

    def landed(chunk, source):
        pltpu.make_async_remote_copy(
            src_ref=slot(chunk, source),
            dst_ref=slot(chunk, source),
            send_sem=w_send.at[2, chunk, z],
            recv_sem=w_recv.at[chunk, source],
            device_id={"fsdp": sibling},
            device_id_type=MESH,
        ).wait_recv()

    def send_own(chunk, carry):
        @pl.when(z < lines - 1)
        def _():
            hop(0, chunk, z, mine + 2, True).start()

        @pl.when(z > 0)
        def _():
            hop(1, chunk, z, mine - 2, True).start()

        return carry

    for chunk in range(chunks):
        send_own(chunk, 0)

    def send_own_core(chunk, carry):
        hop(2, chunk, z, sibling, True).start()
        return carry


    def exchange(phase, source_of, target):
        copies = []
        for d in range(1, n_table):
            peer = lax.rem(me + d, n_table)
            copy = pltpu.make_async_remote_copy(
                src_ref=source_of(peer),
                dst_ref=target,
                send_sem=t_send.at[phase, d],
                recv_sem=t_recv.at[phase, d],
                device_id={"table": peer},
                device_id_type=MESH,
            )
            copy.start()
            copies.append(copy)
        return copies

    loads[0].wait()
    for d in range(n_table):
        req_row[:, d * slot_cap : (d + 1) * slot_cap] = req_ref[0, 0, d : d + 1, :]
    row_ids = lax.broadcasted_iota(jnp.int32, (row_count, slots), 0)
    pick[...] = jnp.where(row_ids == req_row[...], 1.0, 0.0).astype(BF16)
    loads[1].wait()
    received[me] = (
        contract(pick[...], table_ref[0], 0, 0).astype(BF16).reshape(n_table, slot_cap, emb)
    )
    first = exchange(0, lambda peer: received.at[me], received.at[me])
    loads[2].wait()
    loads[3].wait()
    quads = bag_rows.shape[0]
    per_row = samples // quads
    width = per_row * pad
    bag_rows[...] = jnp.full(bag_rows.shape, -1, jnp.int32)
    for s in range(samples):
        at = (s % per_row) * pad
        bag_rows[s // per_row, 0:depth, at : at + feats] = bag_ref[0, s]
    by_sample = jnp.concatenate([bag_rows[g] for g in range(quads)], axis=1)
    total_width = quads * width
    source = lax.broadcasted_iota(jnp.int32, (total_width, total_width), 0)
    target = lax.broadcasted_iota(jnp.int32, (total_width, total_width), 1)
    moves = (target % samples) * pad + target // samples == source
    by_feature = contract(
        by_sample.astype(F32).astype(BF16), jnp.where(moves, 1.0, 0.0).astype(BF16), 1, 0
    )
    used = lax.broadcasted_iota(jnp.int32, by_feature.shape, 1) < feats * samples
    bag_slots[me] = jnp.where(used, by_feature, -1.0)
    second = exchange(1, lambda peer: bag_slots.at[me], bag_slots.at[me])

    for chunk in range(chunks):
        send_own_core(chunk, 0)
    plan[...] = jnp.zeros(plan.shape, jnp.int32)
    feat_ids = lax.broadcasted_iota(jnp.int32, (plan.shape[0] - 8, pattern_ref.shape[1]), 0)
    inverse = jnp.full(feat_ids.shape, per_block, jnp.int32)
    for i in range(per_block):
        inverse = jnp.where(feat_ids == pattern_ref[i : i + 1, :], i, inverse)
    plan[0 : plan.shape[0] - 8, 0 : pattern_ref.shape[1]] = inverse
    plan[plan.shape[0] - 8 : plan.shape[0] - 8 + per_block, 0 : pattern_ref.shape[1]] = pattern_ref[
        ...
    ]
    to_scalar = pltpu.make_async_copy(plan, plan_s, local_sem.at[2])
    to_scalar.start()
    products[:, per_block] = jnp.zeros((products.shape[0], group, emb), F32)
    total[...] = jnp.zeros(total.shape, F32)

    for copy in second:
        copy.wait_recv()
    slot_ids = lax.broadcasted_iota(jnp.int32, (slots, width), 0).astype(F32)

    def count(d, carry):
        for g in range(quads):
            rows = bag_slots[d, :, g * width : (g + 1) * width]
            found = jnp.zeros((slots, width), F32)
            for k in range(depth):
                found = found + jnp.where(slot_ids == rows[k : k + 1, :], 1.0, 0.0)
            counts[d, :, g * width : (g + 1) * width] = found.astype(BF16)
        return carry

    lax.fori_loop(0, n_table, count, 0)
    for copy in first:
        copy.wait_recv()

    def pool(d, carry):
        rows = jnp.concatenate([received[o, d] for o in range(n_table)], axis=0)
        values = contract(counts[d], rows, 0, 0).astype(BF16)
        at = pl.ds(pl.multiple_of(d * samples, samples), samples)
        pooled[:, at, :] = values[: feats * samples].reshape(feats, samples, emb)
        return carry

    to_scalar.wait()
    own_cot.wait()

    def arrive(chunk, distance):
        @pl.when(z >= distance)
        def _():
            landed(chunk, mine - 2 * distance)

            @pl.when(z < lines - 1)
            def _():
                hop(0, chunk, z - distance, mine + 2).start()

            hop(2, chunk, z - distance, sibling).start()

        @pl.when(z + distance < lines)
        def _():
            landed(chunk, mine + 2 * distance)

            @pl.when(z > 0)
            def _():
                hop(1, chunk, z + distance, mine - 2).start()

            hop(2, chunk, z + distance, sibling).start()

    for distance in range(1, lines - 1):
        for chunk in range(chunks):
            arrive(chunk, distance)

    lax.fori_loop(0, n_table, pool, 0)

    def work(chunk, carry):
        arrive(chunk, lines - 1)
        for line in range(lines):
            landed(chunk, 2 * line + 1 - core)
        blocks = range(starts[chunk], starts[chunk + 1])
        step = len(blocks)
        weights = [w[n].reshape(per_block * emb, emb) for n in blocks]
        pres = []
        for b, n in enumerate(blocks):
            picked = jnp.concatenate(
                [
                    pooled[plan_s[plan.shape[0] - 8 + i, me * col_blocks + n]]
                    for i in range(per_block)
                ],
                axis=1,
            )
            pres.append(contract(picked, weights[b], 1, 0))
        grads = []
        for n, pre in zip(blocks, pres):
            sig = jax.nn.sigmoid(pre)
            columns = slice(n * emb, (n + 1) * emb)
            act[:, columns] = (pre * sig).astype(BF16)
            up = cot[:, columns].astype(F32)
            grads.append((up * sig * (1.0 + pre * (1.0 - sig))).astype(BF16))
        for b in range(step):
            back_rows = contract(grads[b], weights[b], 1, 1)
            for i in range(per_block):
                products[b, i] = back_rows[:, i * emb : (i + 1) * emb]

        def add(j, c):
            value = products[0, plan_s[j, me * col_blocks + blocks[0]]]
            for b in range(1, step):
                value = value + products[b, plan_s[j, me * col_blocks + blocks[b]]]
            total[j] = total[j] + value
            return c

        lax.fori_loop(0, feats, add, 0, unroll=True)
        return carry

    for chunk in range(chunks):
        work(chunk, 0)
    act_out = pltpu.make_async_copy(act, act_ref.at[0], local_sem.at[3])
    act_out.start()

    for d in range(n_table):
        rows = total[:, d * samples : (d + 1) * samples, :].astype(BF16)
        rows = rows.reshape(feats * samples, emb)
        slot_grads = contract(counts[d, :, 0 : feats * samples], rows, 1, 0).astype(BF16)
        for o in range(n_table):
            back[o, d] = slot_grads[o * slot_cap : (o + 1) * slot_cap]
    third = exchange(2, lambda peer: back.at[peer], back_in.at[me])
    back_in[me] = back[me]
    for copy in third:
        copy.wait_recv()
    summed = back_in[0].astype(F32)
    for t in range(1, n_table):
        summed = summed + back_in[t].astype(F32)
    summed = summed.reshape(slots, emb)
    high = summed.astype(BF16)
    low = (summed - high.astype(F32)).astype(BF16)
    rows_ref[0] = contract(pick[...], high, 1, 0) + contract(pick[...], low, 1, 0)

    for copies in (first, second, third):
        for copy in copies:
            copy.wait_send()

    def sent_all(chunk, carry):
        for line in range(lines):
            hop(2, chunk, line, sibling).wait_send()

            @pl.when((line <= z) & (z < lines - 1))
            def _():
                hop(0, chunk, line, mine + 2).wait_send()

            @pl.when((line >= z) & (z > 0))
            def _():
                hop(1, chunk, line, mine - 2).wait_send()

        return carry

    for chunk in range(chunks):
        sent_all(chunk, 0)
    act_out.wait()


def fused(n_table, n_fsdp, table_rows, requests, bag_slots, pattern, tiles, cotangent):
    col_blocks, per_block, tile_rows, emb = tiles.shape
    group = cotangent.shape[1]
    row_count = table_rows.shape[1]
    samples, feats, depth = bag_slots.shape[1:]
    slot_cap = requests.shape[3]
    slots = n_table * slot_cap
    lines = n_fsdp // 2
    starts = tuple(round(col_blocks * cut) for cut in CUTS)
    longest = max(b - a for a, b in zip(starts, starts[1:]))
    chunks = len(starts) - 1
    pad = 32
    per_row = 128 // pad
    plan_rows = pad + 8
    vmem, anywhere = pl.BlockSpec(memory_space=pltpu.VMEM), pl.BlockSpec(memory_space=pl.ANY)
    hbm = pl.BlockSpec(memory_space=pltpu.HBM)
    bags = jnp.swapaxes(bag_slots, 2, 3)
    return pl.pallas_call(
        functools.partial(body, n_table, n_fsdp, starts),
        out_shape=(
            jax.ShapeDtypeStruct((1, group, col_blocks * emb), BF16),
            jax.ShapeDtypeStruct((1, row_count, emb), F32),
        ),
        in_specs=[hbm] * 6,
        out_specs=(anywhere, vmem),
        scratch_shapes=[
            pltpu.VMEM(table_rows.shape, BF16),
            pltpu.VMEM(requests.shape, jnp.int32),
            pltpu.VMEM(bags.shape, jnp.int32),
            pltpu.VMEM(pattern.shape[::-1], jnp.int32),
            pltpu.VMEM((col_blocks, per_block, tile_rows * n_fsdp, emb), BF16),
            pltpu.VMEM((group, col_blocks * emb), BF16),
            pltpu.VMEM((group, col_blocks * emb), BF16),
            pltpu.VMEM((1, slots), jnp.int32),
            pltpu.VMEM((samples // per_row, 8, per_row * pad), jnp.int32),
            pltpu.VMEM((n_table, 8, samples * pad), F32),
            pltpu.VMEM((row_count, slots), BF16),
            pltpu.VMEM((n_table, slots, samples * pad), BF16),
            pltpu.VMEM((n_table, n_table, slot_cap, emb), BF16),
            pltpu.VMEM((feats, group, emb), F32),
            pltpu.VMEM((feats, group, emb), BF16),
            pltpu.VMEM((longest, per_block + 1, group, emb), F32),
            pltpu.VMEM((n_table, n_table, slot_cap, emb), BF16),
            pltpu.VMEM((n_table, n_table, slot_cap, emb), BF16),
            pltpu.VMEM((plan_rows, 128), jnp.int32),
            pltpu.SMEM((plan_rows, 128), jnp.int32),
            pltpu.SemaphoreType.DMA((4,)),
            pltpu.SemaphoreType.DMA((4,)),
            pltpu.SemaphoreType.DMA((3, chunks, lines)),
            pltpu.SemaphoreType.DMA((chunks, n_fsdp)),
            pltpu.SemaphoreType.DMA((3, n_table)),
            pltpu.SemaphoreType.DMA((3, n_table)),
        ],
        compiler_params=pltpu.CompilerParams(
            collective_id=0, has_side_effects=True, vmem_limit_bytes=VMEM_LIMIT
        ),
    )(
        table_rows,
        requests,
        bags,
        pattern.T,
        tiles,
        cotangent,
    )


def solution(mesh):
    n_table, n_fsdp = mesh.shape["table"], mesh.shape["fsdp"]
    in_specs = (
        P("fsdp", "table", None),
        P("fsdp", "table", None, None),
        P("fsdp", "table", None, None),
        P(),
        P("table", None, "fsdp", None),
        P("fsdp", None, "table"),
    )
    out_specs = (P("fsdp", None, "table"), P("fsdp", "table", None))

    def program(table_rows, requests, bag_slots, pattern, tiles, cotangent):
        col_blocks, _, tile_rows, emb = tiles.shape
        samples, feats = bag_slots.shape[1:3]
        whole = (
            tile_rows % TILE_ROWS == 0
            and samples % TILE_ROWS == 0
            and emb == 128
            and n_table * requests.shape[3] == 128
            and feats <= 32
            and bag_slots.shape[3] <= 8
            and n_fsdp % 2 == 0
            and col_blocks % 16 == 0
        )
        if whole:
            run = functools.partial(fused, n_table, n_fsdp)
        else:
            run = local
        return run(table_rows, requests, bag_slots, pattern, tiles, cotangent)

    return jax.shard_map(program, mesh=mesh, in_specs=in_specs, out_specs=out_specs, check_vma=False)
```
